256 devices in a mesh: doc: 4 (over y), span: 8 (over z_lo, core), tp: 8 (over x, z_hi).
Axes of the slice: x: 4, y: 4, z: 8 (z_hi: 2, z_lo: 4; z = z_hi * 4 + z_lo), core: 2. Of those that a mesh axis runs over, the one named last changes fastest.
Arguments:
- encoded: bfloat16 [32768, 1024], P(('doc', 'span', 'tp')), may hold values from -12 to 12
- span_lens: int32 [512], P(('doc', 'span')), may hold values from 1 to 64, as said below
- kv_weight: bfloat16 [1024, 8, 256], P(None, 'tp'), may hold values from -0.1875 to 0.1875
- queries: bfloat16 [1024, 8, 1024], P(('doc', 'span'), 'tp'), may hold values from -80 to 80
- out_weight: bfloat16 [8, 1024, 8192], P('tp', None, ('doc', 'span')), may hold values from -0.375 to 0.375
- residual: bfloat16 [1024, 8192], P('tp', ('doc', 'span')), may hold values from -6 to 6
Outputs:
- mixed: bfloat16 [1024, 8192], P('tp', ('doc', 'span'))
The draws below stay inside these ranges and needn't reach their ends.
Inputs may be any that keep to these rules, and one draw needn't show every extreme that they name: `span_lens`: the first span has all 64 rows valid.
All inputs are finite; a program needn't handle non-finite values.
Results may differ from the reference program's by a relative error of at most 0.019.
The reference program's roundings to bfloat16 on the way (of `projected`, `probs` and `attended`) count: a program that leaves them out, or rounds other values in their place, can miss the bound.
Values may be sent and summed in bfloat16 or wider, within the bound.
No kernel may reach another device: no remote copies, remote signals or barrier semaphores. Data moves between devices by JAX's collectives and lax.ppermute only.
A program may use at most 64 MiB of HBM per device.

```python
import math
import jax
import jax.numpy as jnp
from jax import lax

D = 8192
E = 1024
KVH = 8
GROUP = 8
HD = 128
SPAN = 64
ENC_TOK = 32768
NCHUNKS = 512
DEC = 1024


def draw_encoded(key, part):
    key = jax.random.fold_in(key, 5)
    return jnp.clip(jax.random.normal(key, (ENC_TOK, E), jnp.float32), -6.0, 6.0).astype(jnp.bfloat16)


def draw_queries(key, part):
    key = jax.random.fold_in(key, 11)
    return jnp.clip(jax.random.normal(key, (DEC, KVH, GROUP * HD), jnp.float32) * 2.5, -10.0, 10.0).astype(jnp.bfloat16)


def draw_span_lens(key, part):
    key = jax.random.fold_in(key, 17)
    counts = jax.random.randint(key, (NCHUNKS,), 1, SPAN + 1, dtype=jnp.int32)
    return counts.at[0].set(SPAN)


def shard_levels(own_key, extent, cuts, smallest, largest):
    def one(axis_at, parts):
        steps = jax.random.uniform(jax.random.fold_in(jax.random.fold_in(own_key, 6), axis_at), (parts,), jnp.float32, smallest / len(cuts), largest / len(cuts))
        return jnp.repeat(jnp.exp(steps), extent[axis_at] // parts).reshape((-1,) + (1,) * (len(extent) - axis_at - 1))

    gain = one(*cuts[0])
    for cut in cuts[1:]:
        gain = gain * one(*cut)
    return gain


def noise(rng, shape, deviation, limit, cuts=(), held_as=jnp.bfloat16):
    gain = shard_levels(rng, shape, cuts, -0.22, 0.18) if cuts else 1.0
    array = jax.random.normal(rng, shape, jnp.float32) * deviation * gain
    return jnp.minimum(jnp.maximum(array, -limit), limit).astype(held_as)


def setup_inputs(seed: int = 0) -> dict:
    arg_keys = jax.random.split(jax.random.key(seed), 7)
    encoded = draw_encoded(jax.random.fold_in(arg_keys[6], 71), 0)
    span_lens = draw_span_lens(jax.random.fold_in(arg_keys[6], 71), 0)
    kv_weight = noise(arg_keys[2], (E, KVH, 2 * HD), E ** -0.5, 0.1875, ((1, 8),))
    queries = draw_queries(jax.random.fold_in(arg_keys[6], 71), 0)
    out_weight = noise(arg_keys[4], (KVH, GROUP * HD, D), (D // 32) ** -0.5, 0.375, ((0, 8), (2, 32)))
    residual = noise(arg_keys[5], (DEC, D), 1.0, 6.0, ((0, 8), (1, 32)))
    return dict(encoded=encoded, span_lens=span_lens, kv_weight=kv_weight, queries=queries, out_weight=out_weight, residual=residual)


masked_score = -1e30


def reference(encoded, span_lens, kv_weight, queries, out_weight, residual):
    projected = jnp.dot(encoded, kv_weight.reshape(E, KVH * 2 * HD), preferred_element_type=jnp.float32).astype(jnp.bfloat16)
    pairs = projected.reshape(ENC_TOK, KVH, 2, HD)
    keys_all = jnp.transpose(pairs[:, :, 0], (1, 0, 2))
    values_all = jnp.transpose(pairs[:, :, 1], (1, 0, 2))
    position = jnp.arange(ENC_TOK, dtype=jnp.int32) % SPAN
    valid = position < jnp.repeat(span_lens, SPAN)
    query_all = jnp.transpose(queries.reshape(DEC, KVH, GROUP, HD), (1, 0, 2, 3)).reshape(KVH, DEC * GROUP, HD)
    qblock = math.gcd(DEC * GROUP, 512)
    scale = HD ** -0.5

    def per_head(inputs):
        query_head, keys_head, values_head = inputs

        def per_block(query_block):
            scores = jnp.dot(query_block, keys_head.T, preferred_element_type=jnp.float32) * scale
            scores = jnp.where(valid[None, :], scores, masked_score)
            top = jnp.max(scores, axis=-1, keepdims=True)
            probs = jnp.exp(scores - top)
            totals = jnp.sum(probs, axis=-1, keepdims=True)
            weighted = jnp.dot(probs.astype(jnp.bfloat16), values_head, preferred_element_type=jnp.float32)
            return (weighted / totals).astype(jnp.bfloat16)

        blocks = query_head.reshape(DEC * GROUP // qblock, qblock, HD)
        return lax.map(per_block, blocks).reshape(DEC * GROUP, HD)

    attended = lax.map(per_head, (query_all, keys_all, values_all))
    attended = jnp.transpose(attended.reshape(KVH, DEC, GROUP * HD), (1, 0, 2))
    projected_out = jnp.einsum("rhf,hfd->rd", attended.astype(jnp.float32), out_weight.astype(jnp.float32))
    return (residual.astype(jnp.float32) + projected_out).astype(jnp.bfloat16)
```

```python
import functools

import jax
import jax.numpy as jnp
from jax import lax
from jax.experimental import pallas as pl
from jax.experimental.pallas import tpu as pltpu
from jax.sharding import PartitionSpec as P

SPAN = 64
HD = 128
GROUP = 8
AXES = ("doc", "span", "tp")
EXP2_SCALE = HD**-0.5 * 1.4426950408889634
f32, bf16 = jnp.float32, jnp.bfloat16


def move(value, target):
    def index(y, z, c, x, h):
        return ((y % 4 * 4 + z % 4) * 2 + c % 2) * 8 + x % 4 * 2 + h % 2

    pairs = [
        (index(y, z, c, x, h), index(*target(y, z, c, x, h)))
        for y in range(4)
        for z in range(4)
        for c in range(2)
        for x in range(4)
        for h in range(2)
    ]
    return lax.ppermute(value, AXES, pairs)


def from_x(value, k):
    return move(value, lambda y, z, c, x, h: (y, z, c, x - k, h))


def from_y(value, k):
    return move(value, lambda y, z, c, x, h: (y - k, z, c, x, h))


def from_z(value, k):
    return move(value, lambda y, z, c, x, h: (y, z - k, c, x, h))


def other_core(value):
    return move(value, lambda y, z, c, x, h: (y, z, c + 1, x, h))


def other_half(value):
    return move(value, lambda y, z, c, x, h: (y, z, c, x, h + 1))


def vmem(count):
    return [pl.BlockSpec(memory_space=pltpu.VMEM)] * count


SMEM = pl.BlockSpec(memory_space=pltpu.SMEM)
PARAMS = pltpu.CompilerParams(vmem_limit_bytes=40 * 1024 * 1024)


def cost(flops, nbytes, exps=0):
    return pl.CostEstimate(flops=flops, bytes_accessed=nbytes, transcendentals=exps)


def span_pair(place_ref, lens_ref, k, flip):
    x = place_ref[1]
    h = place_ref[2]
    half = (1 - h) if flip else h
    return (lax.rem(x + k, 4) * 2 + half) * 2


def project_kernel(flip, place_ref, lens_ref, e0, e1, e2, e3, weight, out):
    rows = lax.broadcasted_iota(jnp.int32, (SPAN, HD), 0)
    for k, block in enumerate((e0, e1, e2, e3)):
        both = jnp.dot(block[...], weight[...], preferred_element_type=f32)
        first = span_pair(place_ref, lens_ref, k, flip)
        for s in range(2):
            part = both[s * SPAN : (s + 1) * SPAN]
            valid = rows < lens_ref[first + s]
            keys = part[:, :HD]
            keys = jnp.where(valid, keys, keys[:1])
            values = jnp.where(valid, part[:, HD:], 0.0)
            at = k * 2 * SPAN + s * SPAN
            out[at : at + SPAN, :HD] = keys.astype(bf16)
            out[at : at + SPAN, HD:] = values.astype(bf16)


def project(flip, place, lens, blocks, weight):
    return pl.pallas_call(
        functools.partial(project_kernel, flip),
        out_shape=jax.ShapeDtypeStruct((512, 2 * HD), bf16),
        in_specs=[SMEM, SMEM] + vmem(5),
        out_specs=vmem(1)[0],
        compiler_params=PARAMS,
        cost_estimate=cost(2 * 512 * 1024 * 256, 2 << 20),
        name="project",
    )(place, lens, *blocks, weight)


def attend_kernel(place_ref, lens_ref, lens_other_ref, q_ref, a0, a1, b0, b1, out, stats, valued):
    rows = lax.broadcasted_iota(jnp.int32, (SPAN, HD), 0)
    parts = (a0, a1, b0, b1)
    for p, part in enumerate(parts):
        which = lens_ref if p < 2 else lens_other_ref
        valued[p * 512 : (p + 1) * 512, :HD] = part[:, HD:]
        for k in range(4):
            first = span_pair(place_ref, which, k, p % 2 == 1)
            for s in range(2):
                at = p * 512 + k * 2 * SPAN + s * SPAN
                valid = rows < which[first + s]
                valued[at : at + SPAN, HD:] = jnp.where(valid, 1.0, 0.0).astype(bf16)
    count = q_ref.shape[0]
    lane = lax.broadcasted_iota(jnp.int32, (count, HD), 1)
    packed = jnp.zeros((count, HD), f32)
    for g in range(0, GROUP, 2):
        q = jnp.concatenate(
            [q_ref[:, g * HD : (g + 1) * HD], q_ref[:, (g + 1) * HD : (g + 2) * HD]], axis=0
        )
        scores = [
            lax.dot_general(
                q, part[:, :HD], (((1,), (1,)), ((), ())), preferred_element_type=f32
            )
            for part in parts
        ]
        top = functools.reduce(
            jnp.maximum, [jnp.max(block, axis=-1, keepdims=True) for block in scores]
        )
        total = jnp.zeros((2 * count, 2 * HD), f32)
        for p, block in enumerate(scores):
            probs = jnp.exp2((block - top) * EXP2_SCALE).astype(bf16)
            total += jnp.dot(
                probs, valued[p * 512 : (p + 1) * 512], preferred_element_type=f32
            )
        for i in range(2):
            here = slice(i * count, (i + 1) * count)
            out[:, (g + i) * HD : (g + i + 1) * HD] = total[here, :HD].astype(bf16)
            packed = jnp.where(lane == g + i, top[here], packed)
            packed = jnp.where(lane == GROUP + g + i, total[here, HD:], packed)
    stats[...] = packed.T[: 2 * GROUP]


def attend(place, lens, lens_other, q, kv):
    count = q.shape[0]
    return pl.pallas_call(
        attend_kernel,
        out_shape=(
            jax.ShapeDtypeStruct((count, GROUP * HD), bf16),
            jax.ShapeDtypeStruct((2 * GROUP, count), f32),
        ),
        in_specs=[SMEM] * 3 + vmem(5),
        out_specs=tuple(vmem(2)),
        scratch_shapes=[pltpu.VMEM((2048, 2 * HD), bf16)],
        compiler_params=PARAMS,
        cost_estimate=cost(4 * 1024 * 2048 * 256, 2 << 20, 1024 * 2048),
        name="attend",
    )(place, lens, lens_other, q, *kv)


def weights_of(stat_list):
    tops = [s[:GROUP] for s in stat_list]
    top = functools.reduce(jnp.maximum, tops)
    factors = [jnp.exp2((t - top) * EXP2_SCALE) for t in tops]
    total = sum(f * s[GROUP:] for f, s in zip(factors, stat_list))
    return factors, top, total


def by_rows(array):
    return jnp.concatenate([array, jnp.zeros((HD - array.shape[0], HD), f32)], axis=0).T


def fold_kernel(p0, p1, p2, p3, s0, s1, s2, s3, o0, o1, o2, o3, stats):
    factors, top, total = weights_of([s[...] for s in (s0, s1, s2, s3)])
    stats[:GROUP] = top
    stats[GROUP:] = total
    factors = [by_rows(f) for f in factors]
    for g in range(GROUP):
        lanes = slice(g * HD, (g + 1) * HD)
        out = sum(
            part[:, lanes].astype(f32) * f[:, g : g + 1]
            for part, f in zip((p0, p1, p2, p3), factors)
        ).astype(bf16)
        for k, o in enumerate((o0, o1, o2, o3)):
            o[:, lanes] = out[k * 32 : (k + 1) * 32]


def fold(parts, stats):
    return pl.pallas_call(
        fold_kernel,
        out_shape=tuple([jax.ShapeDtypeStruct((32, GROUP * HD), bf16)] * 4)
        + (jax.ShapeDtypeStruct((2 * GROUP, HD), f32),),
        in_specs=vmem(8),
        out_specs=tuple(vmem(5)),
        compiler_params=PARAMS,
        cost_estimate=cost(8 * 128 * 1024, 2 << 20),
        name="fold",
    )(*parts, *stats)


def finish_kernel(p0, p1, p2, p3, s0, s1, s2, s3, out):
    stat_list = []
    for k, s in enumerate((s0, s1, s2, s3)):
        rows = by_rows(s[...])[k * 32 : (k + 1) * 32]
        stat_list.append((rows[:, :GROUP], rows[:, GROUP : 2 * GROUP]))
    top = functools.reduce(jnp.maximum, [t for t, _ in stat_list])
    factors = [jnp.exp2((t - top) * EXP2_SCALE) for t, _ in stat_list]
    total = sum(f * t for f, (_, t) in zip(factors, stat_list))
    for g in range(GROUP):
        lanes = slice(g * HD, (g + 1) * HD)
        joint = sum(
            part[:, lanes].astype(f32) * f[:, g : g + 1]
            for part, f in zip((p0, p1, p2, p3), factors)
        )
        out[:, lanes] = (joint / total[:, g : g + 1]).astype(bf16)


def finish(parts, stats):
    return pl.pallas_call(
        finish_kernel,
        out_shape=jax.ShapeDtypeStruct((32, GROUP * HD), bf16),
        in_specs=vmem(8),
        out_specs=vmem(1)[0],
        compiler_params=PARAMS,
        cost_estimate=cost(8 * 32 * 1024, 1 << 19),
        name="finish",
    )(*parts, *stats)


def output_kernel(place_ref, *refs):
    blocks, weights, outs, rows = refs[:8], refs[8:12], refs[12:16], refs[16]
    z, c = place_ref[3], place_ref[4]
    for i, block in enumerate(blocks):
        k, flip = i % 4, i // 4
        core = (1 - c) if flip else c
        at = (lax.rem(z + k, 4) * 2 + core) * 32
        rows[pl.ds(pl.multiple_of(at, 32), 32), :] = block[...]
    for weight, out in zip(weights, outs):
        out[...] = jnp.dot(rows[...], weight[0], preferred_element_type=f32).astype(bf16)


def output_terms(place, blocks, weights):
    return pl.pallas_call(
        output_kernel,
        out_shape=tuple([jax.ShapeDtypeStruct((256, 256), bf16)] * 4),
        in_specs=[SMEM] + vmem(12),
        out_specs=tuple(vmem(4)),
        scratch_shapes=[pltpu.VMEM((256, GROUP * HD), bf16)],
        compiler_params=PARAMS,
        cost_estimate=cost(2 * 256 * 1024 * 1024, 3 << 20),
        name="output",
    )(place, *blocks, *weights)


def sum_kernel(place_ref, t0, t1, t2, t3, mine, other):
    h = place_ref[2]
    for out, half in ((mine, h), (other, 1 - h)):
        at = pl.ds(pl.multiple_of(half * 128, 128), 128)
        out[...] = sum(t[at, :].astype(f32) for t in (t0, t1, t2, t3)).astype(bf16)


def sum_terms(place, terms):
    return pl.pallas_call(
        sum_kernel,
        out_shape=tuple([jax.ShapeDtypeStruct((128, 256), bf16)] * 2),
        in_specs=[SMEM] + vmem(4),
        out_specs=tuple(vmem(2)),
        compiler_params=PARAMS,
        cost_estimate=cost(4 * 256 * 256, 1 << 19),
        name="sum_terms",
    )(place, *terms)


def body(encoded, span_lens, kv_weight, queries, out_weight, residual):
    span, tp = lax.axis_index("span"), lax.axis_index("tp")
    place = jnp.stack(
        [lax.axis_index("doc"), tp // 2, tp % 2, span // 2, span % 2]
    ).astype(jnp.int32)
    weight = kv_weight.reshape(kv_weight.shape[0], 2 * HD)

    swapped = other_half(encoded)
    near = [encoded] + [from_x(encoded, k) for k in (1, 2, 3)]
    local_q = queries.reshape(queries.shape[0], GROUP * HD)
    row_q = jnp.concatenate([local_q] + [from_z(local_q, k) for k in (1, 2, 3)], axis=0)
    all_q = [row_q] + [from_y(row_q, k) for k in (1, 2, 3)]
    far = [swapped] + [from_x(swapped, k) for k in (1, 2, 3)]
    lens_other = other_core(span_lens)

    kv_near = project(False, place, span_lens, near, weight)
    kv_near_other = other_core(kv_near)
    kv_far = project(True, place, span_lens, far, weight)
    kv_far_other = other_core(kv_far)
    kv = (kv_near, kv_far, kv_near_other, kv_far_other)

    parts, stats = [None] * 4, [None] * 4
    for k in (2, 1, 3, 0):
        part, stat = attend(place, span_lens, lens_other, all_q[k], kv)
        if k:
            part, stat = from_y(part, -k), from_y(stat, -k)
        parts[k], stats[k] = part, stat

    *pieces, joint = fold(parts, stats)
    got = [pieces[0]] + [from_z(pieces[k], -k) for k in (1, 2, 3)]
    got_stats = [joint] + [from_z(joint, -k) for k in (1, 2, 3)]
    attended = finish(got, got_stats)

    weights = [
        move(out_weight, lambda y, z, c, x, h, j=j: (y - x - j, z, c, x, h)) for j in range(4)
    ]
    rows = [attended] + [from_z(attended, k) for k in (1, 2, 3)]
    rows = rows + [other_core(r) for r in rows]
    terms = output_terms(place, rows, weights)
    terms = [terms[0]] + [from_x(terms[j], -j) for j in (1, 2, 3)]
    mine, other = sum_terms(place, terms)
    mine = move(mine, lambda y, z, c, x, h: (y + x, z, c, y, h))
    other = move(other, lambda y, z, c, x, h: (y + x, z, c, y, h + 1))
    return (residual.astype(f32) + (mine.astype(f32) + other.astype(f32))).astype(bf16)


def solution(mesh):
    placed = (
        P(("doc", "span", "tp"), None),
        P(("doc", "span")),
        P(None, "tp", None),
        P(("doc", "span"), "tp", None),
        P("tp", None, ("doc", "span")),
        P("tp", ("doc", "span")),
    )
    return jax.shard_map(
        body, mesh=mesh, in_specs=placed, out_specs=P("tp", ("doc", "span")), check_vma=False
    )
```

```python
import functools

import jax
import jax.numpy as jnp
from jax import lax
from jax.experimental import pallas as pl
from jax.experimental.pallas import tpu as pltpu
from jax.sharding import PartitionSpec as P

SPAN = 64
HD = 128
GROUP = 8
AXES = ("doc", "span", "tp")
Z_ORDER = (0, 2, 1, 3)
EXP2_SCALE = HD**-0.5 * 1.4426950408889634
f32, bf16 = jnp.float32, jnp.bfloat16


def move(value, target):
    def index(y, z, c, x, h):
        return ((y % 4 * 4 + z % 4) * 2 + c % 2) * 8 + x % 4 * 2 + h % 2

    pairs = [
        (index(y, z, c, x, h), index(*target(y, z, c, x, h)))
        for y in range(4)
        for z in range(4)
        for c in range(2)
        for x in range(4)
        for h in range(2)
    ]
    return lax.ppermute(value, AXES, pairs)


def from_x(value, k):
    return move(value, lambda y, z, c, x, h: (y, z, c, x - k, h))


def from_y(value, k):
    return move(value, lambda y, z, c, x, h: (y - k, z, c, x, h))


def swap_z(value, step):
    return move(value, lambda y, z, c, x, h: (y, z ^ step, c, x, h))


def other_core(value):
    return move(value, lambda y, z, c, x, h: (y, z, c + 1, x, h))


def other_half(value):
    return move(value, lambda y, z, c, x, h: (y, z, c, x, h + 1))


def vmem(count):
    return [pl.BlockSpec(memory_space=pltpu.VMEM)] * count


ANY = pl.BlockSpec(memory_space=pl.ANY)
SMEM = pl.BlockSpec(memory_space=pltpu.SMEM)
PARAMS = pltpu.CompilerParams(vmem_limit_bytes=40 * 1024 * 1024)


def cost(flops, nbytes, exps=0):
    return pl.CostEstimate(flops=flops, bytes_accessed=nbytes, transcendentals=exps)


def span_pair(place_ref, lens_ref, k, flip):
    x = place_ref[1]
    h = place_ref[2]
    half = (1 - h) if flip else h
    return (lax.rem(x + k, 4) * 2 + half) * 2


def project_kernel(flip, place_ref, lens_ref, e0, e1, e2, e3, weight, *rest):
    out = rest[-1]
    rows = lax.broadcasted_iota(jnp.int32, (SPAN, HD), 0)
    lane = lax.broadcasted_iota(jnp.int32, (16, 2 * HD), 1)
    lens = jnp.zeros((16, 2 * HD), f32)
    for k, block in enumerate((e0, e1, e2, e3)):
        both = jnp.dot(block[...], weight[...], preferred_element_type=f32)
        first = span_pair(place_ref, lens_ref, k, flip)
        for s in range(2):
            part = both[s * SPAN : (s + 1) * SPAN]
            valid = rows < lens_ref[first + s]
            keys = part[:, :HD]
            keys = jnp.where(valid, keys, keys[:1])
            values = jnp.where(valid, part[:, HD:], 0.0)
            at = k * 2 * SPAN + s * SPAN
            out[at : at + SPAN, :HD] = keys.astype(bf16)
            out[at : at + SPAN, HD:] = values.astype(bf16)
            lens = jnp.where(lane == 2 * k + s, lens_ref[first + s].astype(f32), lens)
    out[512:] = lens.astype(bf16)


def project(flip, place, lens, blocks, weight, after=()):
    return pl.pallas_call(
        functools.partial(project_kernel, flip),
        out_shape=jax.ShapeDtypeStruct((528, 2 * HD), bf16),
        in_specs=[SMEM, SMEM] + vmem(5) + [ANY] * len(after),
        out_specs=vmem(1)[0],
        compiler_params=PARAMS,
        cost_estimate=cost(2 * 512 * 1024 * 256, 2 << 20),
        name="project",
    )(place, lens, *blocks, weight, *after)


def split3(value):
    high = value.astype(bf16)
    rest = value - high.astype(f32)
    middle = rest.astype(bf16)
    low = (rest - middle.astype(f32)).astype(bf16)
    return high, middle, low


def put_stats(out, at, stats):
    for i, term in enumerate(split3(stats)):
        out[at : at + 2 * GROUP, i * HD : (i + 1) * HD] = term
    out[at : at + 2 * GROUP, 3 * HD :] = jnp.zeros((2 * GROUP, (GROUP - 3) * HD), bf16)


def get_stats(part, at):
    terms = [part[at : at + 2 * GROUP, i * HD : (i + 1) * HD].astype(f32) for i in range(3)]
    return (terms[0] + terms[1]) + terms[2]


def attend_kernel(queries, parts, carries, valued, emit):
    rows = lax.broadcasted_iota(jnp.int32, (SPAN, HD), 0).astype(f32)
    for p, part in enumerate(parts):
        valued[p * 512 : (p + 1) * 512, :HD] = part[:512, HD:]
        lens = part[512:, :HD].astype(f32)
        for i in range(8):
            at = p * 512 + i * SPAN
            valid = rows < lens[:1, i : i + 1]
            valued[at : at + SPAN, HD:] = jnp.where(valid, 1.0, 0.0).astype(bf16)
    count = queries[0].shape[0]
    lane = lax.broadcasted_iota(jnp.int32, (count, HD), 1)
    step = 4
    tiles = [(i, g) for i in range(len(queries)) for g in range(0, GROUP, step)]

    def scores_of(i, g):
        q = jnp.concatenate(
            [queries[i][:, h * HD : (h + 1) * HD] for h in range(g, g + step)], axis=0
        )
        return [
            lax.dot_general(
                q, part[:512, :HD], (((1,), (1,)), ((), ())), preferred_element_type=f32
            )
            for part in parts
        ]

    ahead = scores_of(*tiles[0])
    for n, (i, g) in enumerate(tiles):
        scores = ahead
        if n + 1 < len(tiles):
            ahead = scores_of(*tiles[n + 1])
        if g == 0:
            packed = jnp.zeros((count, HD), f32)
            sums = [None] * GROUP
        top = functools.reduce(
            jnp.maximum,
            [block[:, a : a + HD] for block in scores for a in range(0, 512, HD)],
        )
        top = jnp.max(top, axis=-1, keepdims=True)
        if carries[i] is not None:
            before, before_stats = carries[i]
            old = jnp.concatenate([before_stats[:, h : h + 1] for h in range(g, g + step)], axis=0)
            top = jnp.maximum(top, old)
            shrink = jnp.exp2((old - top) * EXP2_SCALE)
        total = jnp.zeros((step * count, 2 * HD), f32)
        for p, block in enumerate(scores):
            probs = jnp.exp2((block - top) * EXP2_SCALE).astype(bf16)
            total += jnp.dot(
                probs, valued[p * 512 : (p + 1) * 512], preferred_element_type=f32
            )
        for j in range(step):
            h = g + j
            here = slice(j * count, (j + 1) * count)
            summed, weight = total[here, :HD], total[here, HD:]
            if carries[i] is not None:
                summed += before[:, h * HD : (h + 1) * HD] * shrink[here]
                weight += before_stats[:, GROUP + h : GROUP + h + 1] * shrink[here]
            sums[h] = summed
            packed = jnp.where(lane == h, top[here], packed)
            packed = jnp.where(lane == GROUP + h, weight, packed)
        if g + step == GROUP:
            emit(i, sums, packed)


def near_kernel(q0, q1, q2, q3, n0, n1, n2, n3, q_all, sums_all, stats_all, valued):
    queries = (q0, q1, q2, q3)
    for i, q in enumerate(queries):
        q_all[i] = q[...]

    def emit(i, sums, packed):
        for h, value in enumerate(sums):
            sums_all[i, :, h * HD : (h + 1) * HD] = value
        stats_all[i] = packed

    attend_kernel(queries, (n0, n1, n2, n3), (None,) * 4, valued, emit)


def attend_near(queries, kv):
    count = queries[0].shape[0]
    return pl.pallas_call(
        near_kernel,
        out_shape=(
            jax.ShapeDtypeStruct((4, count, GROUP * HD), bf16),
            jax.ShapeDtypeStruct((4, count, GROUP * HD), f32),
            jax.ShapeDtypeStruct((4, count, HD), f32),
        ),
        in_specs=vmem(8),
        out_specs=tuple(vmem(3)),
        scratch_shapes=[pltpu.VMEM((2048, 2 * HD), bf16)],
        compiler_params=PARAMS,
        cost_estimate=cost(4 * 2048 * 2048 * 256, 3 << 20, 2048 * 2048),
        name="attend_near",
    )(*queries, *kv)


def far_kernel(k, place_ref, q_all, n0, n1, n2, n3, sums_all, stats_all, out, valued):
    count = q_all.shape[1]
    at = lax.rem(place_ref[1] + k, 4)

    def emit(i, sums, packed):
        for h, value in enumerate(sums):
            out[:count, h * HD : (h + 1) * HD] = value.astype(bf16)
        packed = jnp.concatenate([packed, jnp.zeros((HD - count, HD), f32)], axis=0)
        put_stats(out, count, packed.T[: 2 * GROUP])

    carry = (sums_all.at[at], stats_all[at])
    attend_kernel((q_all.at[at],), (n0, n1, n2, n3), (carry,), valued, emit)


def attend_far(k, place, carries, kv):
    q_all, sums_all, stats_all = carries
    count = q_all.shape[1]
    return pl.pallas_call(
        functools.partial(far_kernel, k),
        out_shape=jax.ShapeDtypeStruct((count + 2 * GROUP, GROUP * HD), bf16),
        in_specs=[SMEM] + vmem(7),
        out_specs=vmem(1)[0],
        scratch_shapes=[pltpu.VMEM((2048, 2 * HD), bf16)],
        compiler_params=PARAMS,
        cost_estimate=cost(4 * 512 * 2048 * 256, 2 << 20, 512 * 2048),
        name="attend_far",
    )(place, q_all, *kv, sums_all, stats_all)


def by_rows(array):
    return jnp.concatenate([array, jnp.zeros((HD - array.shape[0], HD), f32)], axis=0).T


def fold_kernel(count, last, *refs):
    parts, out = refs[:-1], refs[-1]
    stats = [get_stats(part, count) for part in parts]
    half = count // 2
    if last:
        lane = lax.broadcasted_iota(jnp.int32, stats[1].shape, 1)
        ahead, back = (pltpu.roll(stats[1], r, axis=1) for r in (HD - half, half))
        stats[1] = jnp.where(lane < half, ahead, back)
    tops = [s[:GROUP] for s in stats]
    top = functools.reduce(jnp.maximum, tops)
    factors = [jnp.exp2((t - top) * EXP2_SCALE) for t in tops]
    total = sum(f * s[GROUP:] for f, s in zip(factors, stats))
    if last:
        factors = [f / total for f in factors]
    else:
        put_stats(out, count, jnp.concatenate([top, total], axis=0))
    factors = [by_rows(f)[:count] for f in factors]
    for g in range(GROUP):
        lanes = slice(g * HD, (g + 1) * HD)
        pieces = [part[:count, lanes].astype(f32) for part in parts]
        if last:
            pieces[1] = jnp.concatenate([pieces[1][half:], pieces[1][:half]], axis=0)
        out[:count, lanes] = sum(
            piece * f[:, g : g + 1] for piece, f in zip(pieces, factors)
        ).astype(bf16)


def fold(count, parts, last=False):
    return pl.pallas_call(
        functools.partial(fold_kernel, count, last),
        out_shape=jax.ShapeDtypeStruct((count + (0 if last else 2 * GROUP), GROUP * HD), bf16),
        in_specs=vmem(len(parts)),
        out_specs=vmem(1)[0],
        compiler_params=PARAMS,
        cost_estimate=cost(8 * count * 1024, len(parts) * count << 11),
        name="fold",
    )(*parts)


def output_kernel(place_ref, own, beside, other, weights, o0, o1, o2, o3, rows):
    y, z, c = place_ref[0], place_ref[3], place_ref[4]
    blocks = [own.at[:32], own.at[32:], beside.at[:32], beside.at[32:]]
    blocks += [other.at[i * 32 : (i + 1) * 32] for i in range(4)]
    for i, block in enumerate(blocks):
        core = (1 - c) if i >= 4 else c
        at = (jnp.bitwise_xor(z, Z_ORDER[i % 4]) * 2 + core) * 32
        rows[pl.ds(pl.multiple_of(at, 32), 32), :] = block[...]
    for j, out in enumerate((o0, o1, o2, o3)):
        weight = weights[lax.rem(y + j, 4)]
        out[...] = jnp.dot(rows[...], weight, preferred_element_type=f32).astype(bf16)


def output_terms(place, own, beside, other, weights):
    return pl.pallas_call(
        output_kernel,
        out_shape=tuple([jax.ShapeDtypeStruct((256, 256), bf16)] * 4),
        in_specs=[SMEM] + vmem(4),
        out_specs=tuple(vmem(4)),
        scratch_shapes=[pltpu.VMEM((256, GROUP * HD), bf16)],
        compiler_params=PARAMS,
        cost_estimate=cost(2 * 256 * 1024 * 1024, 3 << 20),
        name="output",
    )(place, own, beside, other, weights)


def sum_kernel(place_ref, t0, t1, t2, t3, mine, other):
    h = place_ref[2]
    for out, half in ((mine, h), (other, 1 - h)):
        at = pl.ds(pl.multiple_of(half * 128, 128), 128)
        out[...] = sum(t[at, :].astype(f32) for t in (t0, t1, t2, t3)).astype(out.dtype)


def sum_terms(place, terms):
    return pl.pallas_call(
        sum_kernel,
        out_shape=(
            jax.ShapeDtypeStruct((128, 256), f32),
            jax.ShapeDtypeStruct((128, 256), bf16),
        ),
        in_specs=[SMEM] + vmem(4),
        out_specs=tuple(vmem(2)),
        compiler_params=PARAMS,
        cost_estimate=cost(4 * 256 * 256, 1 << 19),
        name="sum_terms",
    )(place, *terms)


def shared_keys(kv):
    beside = swap_z(kv, 1)
    return kv, other_core(kv), beside, other_core(beside)


def body(encoded, span_lens, kv_weight, queries, out_weight, residual):
    span, tp = lax.axis_index("span"), lax.axis_index("tp")
    place = jnp.stack(
        [lax.axis_index("doc"), tp // 2, tp % 2, span // 2, span % 2]
    ).astype(jnp.int32)
    weight = kv_weight.reshape(kv_weight.shape[0], 2 * HD)
    weights = lax.all_gather(out_weight[0], "doc", axis=0)

    swapped = other_half(encoded)
    near = [encoded] + [from_x(encoded, k) for k in (1, 2, 3)]
    row_q, _ = lax.optimization_barrier((queries.reshape(queries.shape[0], GROUP * HD), swapped))
    row_q = jnp.concatenate([row_q, swap_z(row_q, 2)], axis=0)
    all_q = [row_q] + [from_y(row_q, k) for k in (1, 2, 3)]
    far = [swapped] + [from_x(swapped, k) for k in (1, 2, 3)]

    kv_near = shared_keys(project(False, place, span_lens, near, weight))
    carries = attend_near(all_q, kv_near)
    kv_far = project(True, place, span_lens, far, weight)
    beside = swap_z(kv_far, 1)
    beside, carries = lax.optimization_barrier((beside, carries))
    kv_far = kv_far, other_core(kv_far), beside, other_core(beside)

    parts = [None] * 4
    for k in (2, 1, 3, 0):
        part = attend_far(k, place, carries, kv_far)
        parts[k] = from_y(part, -k) if k else part

    joint = fold(64, parts)
    own = fold(64, (joint, swap_z(joint, 2)), last=True)
    beside = swap_z(own, 1)
    other = other_core(jnp.concatenate([own, beside], axis=0))
    terms = output_terms(place, own, beside, other, weights)
    terms = [
        move(term, lambda y, z, c, x, h, j=j: (y + j, z, c, x + y, h))
        for j, term in enumerate(terms)
    ]
    mine, other = sum_terms(place, terms)
    other = other_half(other).astype(f32)
    return (residual.astype(f32) + (mine + other)).astype(bf16)


def solution(mesh):
    placed = (
        P(("doc", "span", "tp"), None),
        P(("doc", "span")),
        P(None, "tp", None),
        P(("doc", "span"), "tp", None),
        P("tp", None, ("doc", "span")),
        P("tp", ("doc", "span")),
    )
    return jax.shard_map(
        body, mesh=mesh, in_specs=placed, out_specs=P("tp", ("doc", "span")), check_vma=False
    )
```

```python
import functools

import jax
import jax.numpy as jnp
from jax import lax
from jax.experimental import pallas as pl
from jax.experimental.pallas import tpu as pltpu
from jax.sharding import PartitionSpec as P

SPAN = 64
HD = 128
GROUP = 8
AXES = ("doc", "span", "tp")
Z_ORDER = (0, 2, 1, 3)
EXP2_SCALE = HD**-0.5 * 1.4426950408889634
f32, bf16 = jnp.float32, jnp.bfloat16


def move(value, target):
    def index(y, z, c, x, h):
        return ((y % 4 * 4 + z % 4) * 2 + c % 2) * 8 + x % 4 * 2 + h % 2

    pairs = [
        (index(y, z, c, x, h), index(*target(y, z, c, x, h)))
        for y in range(4)
        for z in range(4)
        for c in range(2)
        for x in range(4)
        for h in range(2)
    ]
    return lax.ppermute(value, AXES, pairs)


def from_x(value, k):
    return move(value, lambda y, z, c, x, h: (y, z, c, x - k, h))


def from_y(value, k):
    return move(value, lambda y, z, c, x, h: (y - k, z, c, x, h))


def swap_z(value, step):
    return move(value, lambda y, z, c, x, h: (y, z ^ step, c, x, h))


def other_core(value):
    return move(value, lambda y, z, c, x, h: (y, z, c + 1, x, h))


def other_half(value):
    return move(value, lambda y, z, c, x, h: (y, z, c, x, h + 1))


def vmem(count):
    return [pl.BlockSpec(memory_space=pltpu.VMEM)] * count


ANY = pl.BlockSpec(memory_space=pl.ANY)
SMEM = pl.BlockSpec(memory_space=pltpu.SMEM)
PARAMS = pltpu.CompilerParams(vmem_limit_bytes=40 * 1024 * 1024)


def cost(flops, nbytes, exps=0):
    return pl.CostEstimate(flops=flops, bytes_accessed=nbytes, transcendentals=exps)


def span_pair(place_ref, lens_ref, k, flip):
    x = place_ref[1]
    h = place_ref[2]
    half = (1 - h) if flip else h
    return (lax.rem(x + k, 4) * 2 + half) * 2


def project_kernel(flip, place_ref, lens_ref, e0, e1, e2, e3, weight, *rest):
    out = rest[-1]
    rows = lax.broadcasted_iota(jnp.int32, (SPAN, HD), 0)
    lane = lax.broadcasted_iota(jnp.int32, (16, 2 * HD), 1)
    lens = jnp.zeros((16, 2 * HD), f32)
    for k, block in enumerate((e0, e1, e2, e3)):
        both = jnp.dot(block[...], weight[...], preferred_element_type=f32)
        first = span_pair(place_ref, lens_ref, k, flip)
        for s in range(2):
            part = both[s * SPAN : (s + 1) * SPAN]
            valid = rows < lens_ref[first + s]
            keys = part[:, :HD]
            keys = jnp.where(valid, keys, keys[:1])
            values = jnp.where(valid, part[:, HD:], 0.0)
            at = k * 2 * SPAN + s * SPAN
            out[at : at + SPAN, :HD] = keys.astype(bf16)
            out[at : at + SPAN, HD:] = values.astype(bf16)
            lens = jnp.where(lane == 2 * k + s, lens_ref[first + s].astype(f32), lens)
    out[512:] = lens.astype(bf16)


def project(flip, place, lens, blocks, weight, after=()):
    return pl.pallas_call(
        functools.partial(project_kernel, flip),
        out_shape=jax.ShapeDtypeStruct((528, 2 * HD), bf16),
        in_specs=[SMEM, SMEM] + vmem(5) + [ANY] * len(after),
        out_specs=vmem(1)[0],
        compiler_params=PARAMS,
        cost_estimate=cost(2 * 512 * 1024 * 256, 2 << 20) if flip else cost(1024, 1024),
        name="project",
    )(place, lens, *blocks, weight, *after)


def split3(value):
    high = value.astype(bf16)
    rest = value - high.astype(f32)
    middle = rest.astype(bf16)
    low = (rest - middle.astype(f32)).astype(bf16)
    return high, middle, low


def put_stats(out, stats):
    terms = [term.astype(f32) for term in split3(stats)]
    lane = lax.broadcasted_iota(jnp.int32, stats.shape, 1)
    for i in (1, 2):
        shifted = pltpu.roll(terms[i], 2 * GROUP * i, axis=1)
        terms[0] = jnp.where(lane < 2 * GROUP * i, terms[0], shifted)
    out[:, GROUP * HD :] = terms[0].astype(bf16)


def get_stats(part):
    terms = part[:, GROUP * HD :].astype(f32)
    second, third = (pltpu.roll(terms, HD - 2 * GROUP * i, axis=1) for i in (1, 2))
    return (terms + second) + third


def attend_kernel(queries, parts, carries, valued, emit):
    rows = lax.broadcasted_iota(jnp.int32, (SPAN, HD), 0).astype(f32)
    for p, part in enumerate(parts):
        valued[p * 512 : (p + 1) * 512, :HD] = part[:512, HD:]
        lens = part[512:, :HD].astype(f32)
        for i in range(8):
            at = p * 512 + i * SPAN
            valid = rows < lens[:1, i : i + 1]
            valued[at : at + SPAN, HD:] = jnp.where(valid, 1.0, 0.0).astype(bf16)
    count = queries[0].shape[0]
    lane = lax.broadcasted_iota(jnp.int32, (count, HD), 1)
    step = 4
    tiles = [(i, g) for i in range(len(queries)) for g in range(0, GROUP, step)]

    def scores_of(i, g):
        q = jnp.concatenate(
            [queries[i][:, h * HD : (h + 1) * HD] for h in range(g, g + step)], axis=0
        )
        return [
            lax.dot_general(
                q, part[:512, :HD], (((1,), (1,)), ((), ())), preferred_element_type=f32
            )
            for part in parts
        ]

    ahead = scores_of(*tiles[0])
    for n, (i, g) in enumerate(tiles):
        scores = ahead
        if n + 1 < len(tiles):
            ahead = scores_of(*tiles[n + 1])
        if g == 0:
            packed = jnp.zeros((count, HD), f32)
            sums = [None] * GROUP
        top = functools.reduce(
            jnp.maximum,
            [block[:, a : a + HD] for block in scores for a in range(0, 512, HD)],
        )
        top = jnp.max(top, axis=-1, keepdims=True)
        if carries[i] is not None:
            before, before_stats = carries[i]
            old = jnp.concatenate([before_stats[:, h : h + 1] for h in range(g, g + step)], axis=0)
            top = jnp.maximum(top, old)
            shrink = jnp.exp2((old - top) * EXP2_SCALE)
        total = jnp.zeros((step * count, 2 * HD), f32)
        for p, block in enumerate(scores):
            probs = jnp.exp2((block - top) * EXP2_SCALE).astype(bf16)
            total += jnp.dot(
                probs, valued[p * 512 : (p + 1) * 512], preferred_element_type=f32
            )
        for j in range(step):
            h = g + j
            here = slice(j * count, (j + 1) * count)
            summed, weight = total[here, :HD], total[here, HD:]
            if carries[i] is not None:
                summed += before[:, h * HD : (h + 1) * HD] * shrink[here]
                weight += before_stats[:, GROUP + h : GROUP + h + 1] * shrink[here]
            sums[h] = summed
            packed = jnp.where(lane == h, top[here], packed)
            packed = jnp.where(lane == GROUP + h, weight, packed)
        if g + step == GROUP:
            emit(i, sums, packed)


def near_kernel(q0, q1, q2, q3, n0, n1, n2, n3, q_all, sums_all, stats_all, valued):
    queries = (q0, q1, q2, q3)
    for i, q in enumerate(queries):
        q_all[i] = q[...]

    def emit(i, sums, packed):
        for h, value in enumerate(sums):
            sums_all[i, :, h * HD : (h + 1) * HD] = value
        stats_all[i] = packed

    attend_kernel(queries, (n0, n1, n2, n3), (None,) * 4, valued, emit)


def attend_near(queries, kv):
    count = queries[0].shape[0]
    return pl.pallas_call(
        near_kernel,
        out_shape=(
            jax.ShapeDtypeStruct((4, count, GROUP * HD), bf16),
            jax.ShapeDtypeStruct((4, count, GROUP * HD), f32),
            jax.ShapeDtypeStruct((4, count, HD), f32),
        ),
        in_specs=vmem(8),
        out_specs=tuple(vmem(3)),
        scratch_shapes=[pltpu.VMEM((2048, 2 * HD), bf16)],
        compiler_params=PARAMS,
        cost_estimate=cost(1024, 1024),
        name="attend_near",
    )(*queries, *kv)


def far_kernel(k, place_ref, q_all, n0, n1, n2, n3, sums_all, stats_all, out, valued):
    count = q_all.shape[1]
    at = lax.rem(place_ref[1] + k, 4)

    def emit(i, sums, packed):
        for h, value in enumerate(sums):
            out[:, h * HD : (h + 1) * HD] = value.astype(bf16)
        put_stats(out, packed)

    carry = (sums_all.at[at], stats_all[at])
    attend_kernel((q_all.at[at],), (n0, n1, n2, n3), (carry,), valued, emit)


def attend_far(k, place, carries, kv):
    q_all, sums_all, stats_all = carries
    count = q_all.shape[1]
    return pl.pallas_call(
        functools.partial(far_kernel, k),
        out_shape=jax.ShapeDtypeStruct((count, GROUP * HD + HD), bf16),
        in_specs=[SMEM] + vmem(7),
        out_specs=vmem(1)[0],
        scratch_shapes=[pltpu.VMEM((2048, 2 * HD), bf16)],
        compiler_params=PARAMS,
        cost_estimate=cost(4 * 512 * 2048 * 256, 2 << 20, 512 * 2048),
        name="attend_far",
    )(place, q_all, *kv, sums_all, stats_all)


def fold_kernel(last, *refs):
    parts, out = refs[:-1], refs[-1]
    stats = [get_stats(part) for part in parts]
    half = out.shape[0] // 2
    if last:
        stats[1] = jnp.concatenate([stats[1][half:], stats[1][:half]], axis=0)
    top = functools.reduce(jnp.maximum, stats)
    factors = [jnp.exp2((s - top) * EXP2_SCALE) for s in stats]
    shifted = [pltpu.roll(f, GROUP, axis=1) for f in factors]
    total = sum(f * s for f, s in zip(shifted, stats))
    if not last:
        lane = lax.broadcasted_iota(jnp.int32, top.shape, 1)
        put_stats(out, jnp.where(lane < GROUP, top, total))
    for g in range(GROUP):
        lanes = slice(g * HD, (g + 1) * HD)
        pieces = [part[:, lanes].astype(f32) for part in parts]
        if last:
            pieces[1] = jnp.concatenate([pieces[1][half:], pieces[1][:half]], axis=0)
        joint = sum(piece * f[:, g : g + 1] for piece, f in zip(pieces, factors))
        if last:
            joint = joint / total[:, GROUP + g : GROUP + g + 1]
        out[:, lanes] = joint.astype(bf16)


def fold(count, parts, last=False):
    return pl.pallas_call(
        functools.partial(fold_kernel, last),
        out_shape=jax.ShapeDtypeStruct((count, GROUP * HD + (0 if last else HD)), bf16),
        in_specs=vmem(len(parts)),
        out_specs=vmem(1)[0],
        compiler_params=PARAMS,
        cost_estimate=cost(8 * count * 1024, len(parts) * count << 11),
        name="fold",
    )(*parts)


def output_kernel(place_ref, own, beside, other, weights, o0, o1, o2, o3, rows):
    y, z, c = place_ref[0], place_ref[3], place_ref[4]
    blocks = [own.at[:32], own.at[32:], beside.at[:32], beside.at[32:]]
    blocks += [other.at[i * 32 : (i + 1) * 32] for i in range(4)]
    for i, block in enumerate(blocks):
        core = (1 - c) if i >= 4 else c
        at = (jnp.bitwise_xor(z, Z_ORDER[i % 4]) * 2 + core) * 32
        rows[pl.ds(pl.multiple_of(at, 32), 32), :] = block[...]
    for j, out in enumerate((o0, o1, o2, o3)):
        weight = weights[lax.rem(y + j, 4)]
        out[...] = jnp.dot(rows[...], weight, preferred_element_type=f32).astype(bf16)


def output_terms(place, own, beside, other, weights):
    return pl.pallas_call(
        output_kernel,
        out_shape=tuple([jax.ShapeDtypeStruct((256, 256), bf16)] * 4),
        in_specs=[SMEM] + vmem(4),
        out_specs=tuple(vmem(4)),
        scratch_shapes=[pltpu.VMEM((256, GROUP * HD), bf16)],
        compiler_params=PARAMS,
        cost_estimate=cost(2 * 256 * 1024 * 1024, 3 << 20),
        name="output",
    )(place, own, beside, other, weights)


def sum_kernel(place_ref, t0, t1, t2, t3, mine, other):
    h = place_ref[2]
    for out, half in ((mine, h), (other, 1 - h)):
        at = pl.ds(pl.multiple_of(half * 128, 128), 128)
        out[...] = sum(t[at, :].astype(f32) for t in (t0, t1, t2, t3)).astype(out.dtype)


def sum_terms(place, terms):
    return pl.pallas_call(
        sum_kernel,
        out_shape=(
            jax.ShapeDtypeStruct((128, 256), f32),
            jax.ShapeDtypeStruct((128, 256), bf16),
        ),
        in_specs=[SMEM] + vmem(4),
        out_specs=tuple(vmem(2)),
        compiler_params=PARAMS,
        cost_estimate=cost(4 * 256 * 256, 1 << 19),
        name="sum_terms",
    )(place, *terms)


def body(encoded, span_lens, kv_weight, queries, out_weight, residual):
    span, tp = lax.axis_index("span"), lax.axis_index("tp")
    place = jnp.stack(
        [lax.axis_index("doc"), tp // 2, tp % 2, span // 2, span % 2]
    ).astype(jnp.int32)
    weight = kv_weight.reshape(kv_weight.shape[0], 2 * HD)
    weights = lax.all_gather(out_weight[0], "doc", axis=0)

    near = [encoded] + [from_x(encoded, k) for k in (1, 2, 3)]
    swapped = other_half(encoded)
    row_q = queries.reshape(queries.shape[0], GROUP * HD)
    row_q = jnp.concatenate([row_q, swap_z(row_q, 2)], axis=0)
    far = [swapped] + [from_x(swapped, k) for k in (1, 2, 3)]
    all_q = [row_q] + [from_y(row_q, k) for k in (1, 2, 3)]

    kv_near = project(False, place, span_lens, near, weight)
    beside = swap_z(kv_near, 1)
    kv_near = kv_near, other_core(kv_near), beside, other_core(beside)
    carries = attend_near(all_q, kv_near)
    far = lax.optimization_barrier(far + all_q)[:4]
    kv_far = project(True, place, span_lens, far, weight)
    beside = swap_z(kv_far, 1)
    beside, carries, weights = lax.optimization_barrier((beside, carries, weights))
    kv_far = kv_far, other_core(kv_far), beside, other_core(beside)

    parts = [None] * 4
    for k in (2, 1, 3, 0):
        part = attend_far(k, place, carries, kv_far)
        parts[k] = from_y(part, -k) if k else part

    joint = fold(64, parts)
    own = fold(64, (joint, swap_z(joint, 2)), last=True)
    beside = swap_z(own, 1)
    other = other_core(jnp.concatenate([own, beside], axis=0))
    terms = output_terms(place, own, beside, other, weights)
    terms = [
        move(term, lambda y, z, c, x, h, j=j: (y + j, z, c, x + y, h))
        for j, term in enumerate(terms)
    ]
    mine, other = sum_terms(place, terms)
    other = other_half(other).astype(f32)
    return (residual.astype(f32) + (mine + other)).astype(bf16)


def solution(mesh):
    placed = (
        P(("doc", "span", "tp"), None),
        P(("doc", "span")),
        P(None, "tp", None),
        P(("doc", "span"), "tp", None),
        P("tp", None, ("doc", "span")),
        P("tp", ("doc", "span")),
    )
    return jax.shard_map(
        body, mesh=mesh, in_specs=placed, out_specs=P("tp", ("doc", "span")), check_vma=False
    )
```

```python
import functools

import jax
import jax.numpy as jnp
from jax import lax
from jax.experimental import pallas as pl
from jax.experimental.pallas import tpu as pltpu
from jax.sharding import PartitionSpec as P

SPAN = 64
HD = 128
GROUP = 8
AXES = ("doc", "span", "tp")
Z_ORDER = (0, 2, 1, 3)
EXP2_SCALE = HD**-0.5 * 1.4426950408889634
f32, bf16 = jnp.float32, jnp.bfloat16


def move(value, target):
    def index(y, z, c, x, h):
        return ((y % 4 * 4 + z % 4) * 2 + c % 2) * 8 + x % 4 * 2 + h % 2

    pairs = [
        (index(y, z, c, x, h), index(*target(y, z, c, x, h)))
        for y in range(4)
        for z in range(4)
        for c in range(2)
        for x in range(4)
        for h in range(2)
    ]
    return lax.ppermute(value, AXES, pairs)


def from_x(value, k):
    return move(value, lambda y, z, c, x, h: (y, z, c, x - k, h))


def from_y(value, k):
    return move(value, lambda y, z, c, x, h: (y - k, z, c, x, h))


def swap_z(value, step):
    return move(value, lambda y, z, c, x, h: (y, z ^ step, c, x, h))


def other_core(value):
    return move(value, lambda y, z, c, x, h: (y, z, c + 1, x, h))


def other_half(value):
    return move(value, lambda y, z, c, x, h: (y, z, c, x, h + 1))


def vmem(count):
    return [pl.BlockSpec(memory_space=pltpu.VMEM)] * count


ANY = pl.BlockSpec(memory_space=pl.ANY)
SMEM = pl.BlockSpec(memory_space=pltpu.SMEM)
PARAMS = pltpu.CompilerParams(vmem_limit_bytes=40 * 1024 * 1024)


def cost(flops, nbytes, exps=0):
    return pl.CostEstimate(flops=flops, bytes_accessed=nbytes, transcendentals=exps)


def span_pair(place_ref, lens_ref, k, flip):
    x = place_ref[1]
    h = place_ref[2]
    half = (1 - h) if flip else h
    return (lax.rem(x + k, 4) * 2 + half) * 2


def project_kernel(flip, place_ref, lens_ref, e0, e1, e2, e3, weight, *rest):
    out = rest[-1]
    rows = lax.broadcasted_iota(jnp.int32, (SPAN, HD), 0)
    lane = lax.broadcasted_iota(jnp.int32, (16, 2 * HD), 1)
    lens = jnp.zeros((16, 2 * HD), f32)
    for k, block in enumerate((e0, e1, e2, e3)):
        both = jnp.dot(block[...], weight[...], preferred_element_type=f32)
        first = span_pair(place_ref, lens_ref, k, flip)
        for s in range(2):
            part = both[s * SPAN : (s + 1) * SPAN]
            valid = rows < lens_ref[first + s]
            keys = part[:, :HD]
            keys = jnp.where(valid, keys, keys[:1])
            values = jnp.where(valid, part[:, HD:], 0.0)
            at = k * 2 * SPAN + s * SPAN
            out[at : at + SPAN, :HD] = keys.astype(bf16)
            out[at : at + SPAN, HD:] = values.astype(bf16)
            lens = jnp.where(lane == 2 * k + s, lens_ref[first + s].astype(f32), lens)
    out[512:] = lens.astype(bf16)


def project(flip, place, lens, blocks, weight, after=()):
    return pl.pallas_call(
        functools.partial(project_kernel, flip),
        out_shape=jax.ShapeDtypeStruct((528, 2 * HD), bf16),
        in_specs=[SMEM, SMEM] + vmem(5) + [ANY] * len(after),
        out_specs=vmem(1)[0],
        compiler_params=PARAMS,
        cost_estimate=cost(2 * 512 * 1024 * 256, 2 << 20) if flip else cost(1024, 1024),
        name="project",
    )(place, lens, *blocks, weight, *after)


def split3(value):
    high = value.astype(bf16)
    rest = value - high.astype(f32)
    middle = rest.astype(bf16)
    low = (rest - middle.astype(f32)).astype(bf16)
    return high, middle, low


def put_stats(out, stats):
    terms = [term.astype(f32) for term in split3(stats)]
    lane = lax.broadcasted_iota(jnp.int32, stats.shape, 1)
    for i in (1, 2):
        shifted = pltpu.roll(terms[i], 2 * GROUP * i, axis=1)
        terms[0] = jnp.where(lane < 2 * GROUP * i, terms[0], shifted)
    out[:, GROUP * HD :] = terms[0].astype(bf16)


def get_stats(part):
    terms = part[:, GROUP * HD :].astype(f32)
    second, third = (pltpu.roll(terms, HD - 2 * GROUP * i, axis=1) for i in (1, 2))
    return (terms + second) + third


def attend_kernel(queries, parts, carries, valued, emit):
    rows = lax.broadcasted_iota(jnp.int32, (SPAN, HD), 0).astype(f32)
    for p, part in enumerate(parts):
        valued[p * 512 : (p + 1) * 512, :HD] = part[:512, HD:]
        lens = part[512:, :HD].astype(f32)
        for i in range(8):
            at = p * 512 + i * SPAN
            valid = rows < lens[:1, i : i + 1]
            valued[at : at + SPAN, HD:] = jnp.where(valid, 1.0, 0.0).astype(bf16)
    count = queries[0].shape[0]
    lane = lax.broadcasted_iota(jnp.int32, (count, HD), 1)
    step = 4
    tiles = [(i, g) for i in range(len(queries)) for g in range(0, GROUP, step)]

    def scores_of(i, g):
        q = jnp.concatenate(
            [queries[i][:, h * HD : (h + 1) * HD] for h in range(g, g + step)], axis=0
        )
        return [
            lax.dot_general(
                q, part[:512, :HD], (((1,), (1,)), ((), ())), preferred_element_type=f32
            )
            for part in parts
        ]

    ahead = scores_of(*tiles[0])
    for n, (i, g) in enumerate(tiles):
        scores = ahead
        if n + 1 < len(tiles):
            ahead = scores_of(*tiles[n + 1])
        if g == 0:
            packed = jnp.zeros((count, HD), f32)
            sums = [None] * GROUP
        top = functools.reduce(
            jnp.maximum,
            [block[:, a : a + HD] for block in scores for a in range(0, 512, HD)],
        )
        top = jnp.max(top, axis=-1, keepdims=True)
        if carries[i] is not None:
            before, before_stats = carries[i]
            old = jnp.concatenate([before_stats[:, h : h + 1] for h in range(g, g + step)], axis=0)
            top = jnp.maximum(top, old)
            shrink = jnp.exp2((old - top) * EXP2_SCALE)
        total = jnp.zeros((step * count, 2 * HD), f32)
        for p, block in enumerate(scores):
            probs = jnp.exp2((block - top) * EXP2_SCALE).astype(bf16)
            total += jnp.dot(
                probs, valued[p * 512 : (p + 1) * 512], preferred_element_type=f32
            )
        for j in range(step):
            h = g + j
            here = slice(j * count, (j + 1) * count)
            summed, weight = total[here, :HD], total[here, HD:]
            if carries[i] is not None:
                summed += before[:, h * HD : (h + 1) * HD] * shrink[here]
                weight += before_stats[:, GROUP + h : GROUP + h + 1] * shrink[here]
            sums[h] = summed
            packed = jnp.where(lane == h, top[here], packed)
            packed = jnp.where(lane == GROUP + h, weight, packed)
        if g + step == GROUP:
            emit(i, sums, packed)


def near_kernel(*refs):
    queries, parts = refs[:4], refs[4:-4]
    q_all, sums_all, stats_all, valued = refs[-4:]
    for i, q in enumerate(queries):
        q_all[i] = q[...]

    def emit(i, sums, packed):
        for h, value in enumerate(sums):
            sums_all[i, :, h * HD : (h + 1) * HD] = value
        stats_all[i] = packed

    attend_kernel(queries, parts, (None,) * 4, valued, emit)


def attend_near(queries, kv):
    count = queries[0].shape[0]
    return pl.pallas_call(
        near_kernel,
        out_shape=(
            jax.ShapeDtypeStruct((4, count, GROUP * HD), bf16),
            jax.ShapeDtypeStruct((4, count, GROUP * HD), f32),
            jax.ShapeDtypeStruct((4, count, HD), f32),
        ),
        in_specs=vmem(4 + len(kv)),
        out_specs=tuple(vmem(3)),
        scratch_shapes=[pltpu.VMEM((512 * len(kv), 2 * HD), bf16)],
        compiler_params=PARAMS,
        cost_estimate=cost(1024, 1024),
        name="attend_near",
    )(*queries, *kv)


def far_kernel(k, place_ref, q_all, sums_all, stats_all, *rest):
    parts, out, valued = rest[:-2], rest[-2], rest[-1]
    count = q_all.shape[1]
    at = lax.rem(place_ref[1] + k, 4)

    def emit(i, sums, packed):
        for h, value in enumerate(sums):
            out[:, h * HD : (h + 1) * HD] = value.astype(bf16)
        put_stats(out, packed)

    carry = (sums_all.at[at], stats_all[at])
    attend_kernel((q_all.at[at],), parts, (carry,), valued, emit)


def attend_far(k, place, carries, kv):
    q_all, sums_all, stats_all = carries
    count = q_all.shape[1]
    return pl.pallas_call(
        functools.partial(far_kernel, k),
        out_shape=jax.ShapeDtypeStruct((count, GROUP * HD + HD), bf16),
        in_specs=[SMEM] + vmem(3 + len(kv)),
        out_specs=vmem(1)[0],
        scratch_shapes=[pltpu.VMEM((512 * len(kv), 2 * HD), bf16)],
        compiler_params=PARAMS,
        cost_estimate=cost(4 * 512 * 1024 * 256, 2 << 20, 512 * 1024),
        name="attend_far",
    )(place, q_all, sums_all, stats_all, *kv)


def fold_kernel(last, *refs):
    parts, out = refs[:-1], refs[-1]
    stats = [get_stats(part) for part in parts]
    half = out.shape[0] // 2
    if last:
        stats[1] = jnp.concatenate([stats[1][half:], stats[1][:half]], axis=0)
    top = functools.reduce(jnp.maximum, stats)
    factors = [jnp.exp2((s - top) * EXP2_SCALE) for s in stats]
    shifted = [pltpu.roll(f, GROUP, axis=1) for f in factors]
    total = sum(f * s for f, s in zip(shifted, stats))
    if not last:
        lane = lax.broadcasted_iota(jnp.int32, top.shape, 1)
        put_stats(out, jnp.where(lane < GROUP, top, total))
    for g in range(GROUP):
        lanes = slice(g * HD, (g + 1) * HD)
        pieces = [part[:, lanes].astype(f32) for part in parts]
        if last:
            pieces[1] = jnp.concatenate([pieces[1][half:], pieces[1][:half]], axis=0)
        joint = sum(piece * f[:, g : g + 1] for piece, f in zip(pieces, factors))
        if last:
            joint = joint / total[:, GROUP + g : GROUP + g + 1]
        out[:, lanes] = joint.astype(bf16)


def fold(count, parts, last=False):
    return pl.pallas_call(
        functools.partial(fold_kernel, last),
        out_shape=jax.ShapeDtypeStruct((count, GROUP * HD + (0 if last else HD)), bf16),
        in_specs=vmem(len(parts)),
        out_specs=vmem(1)[0],
        compiler_params=PARAMS,
        cost_estimate=cost(8 * count * 1024, len(parts) * count << 11),
        name="fold",
    )(*parts)


def output_kernel(place_ref, r0, r1, r2, r3, weights, o0, o1, o2, o3, rows):
    y, z, c = place_ref[0], place_ref[3], place_ref[4]
    blocks = [r.at[i : i + 32] for r in (r0, r1, r2, r3) for i in (0, 32)]
    for i, block in enumerate(blocks):
        core = (1 - c) if i >= 4 else c
        at = (jnp.bitwise_xor(z, Z_ORDER[i % 4]) * 2 + core) * 32
        rows[pl.ds(pl.multiple_of(at, 32), 32), :] = block[...]
    for j, out in enumerate((o0, o1, o2, o3)):
        weight = weights[lax.rem(y + j, 4)]
        out[...] = jnp.dot(rows[...], weight, preferred_element_type=f32).astype(bf16)


def output_terms(place, rows, weights):
    return pl.pallas_call(
        output_kernel,
        out_shape=tuple([jax.ShapeDtypeStruct((256, 256), bf16)] * 4),
        in_specs=[SMEM] + vmem(5),
        out_specs=tuple(vmem(4)),
        scratch_shapes=[pltpu.VMEM((256, GROUP * HD), bf16)],
        compiler_params=PARAMS,
        cost_estimate=cost(2 * 256 * 1024 * 1024, 3 << 20),
        name="output",
    )(place, *rows, weights)


def sum_kernel(place_ref, t0, t1, t2, t3, mine, other):
    h = place_ref[2]
    for out, half in ((mine, h), (other, 1 - h)):
        at = pl.ds(pl.multiple_of(half * 128, 128), 128)
        out[...] = sum(t[at, :].astype(f32) for t in (t0, t1, t2, t3)).astype(out.dtype)


def sum_terms(place, terms):
    return pl.pallas_call(
        sum_kernel,
        out_shape=(
            jax.ShapeDtypeStruct((128, 256), f32),
            jax.ShapeDtypeStruct((128, 256), bf16),
        ),
        in_specs=[SMEM] + vmem(4),
        out_specs=tuple(vmem(2)),
        compiler_params=PARAMS,
        cost_estimate=cost(4 * 256 * 256, 1 << 19),
        name="sum_terms",
    )(place, *terms)


def body(encoded, span_lens, kv_weight, queries, out_weight, residual):
    span, tp = lax.axis_index("span"), lax.axis_index("tp")
    place = jnp.stack(
        [lax.axis_index("doc"), tp // 2, tp % 2, span // 2, span % 2]
    ).astype(jnp.int32)
    weight = kv_weight.reshape(kv_weight.shape[0], 2 * HD)
    weights = lax.all_gather(out_weight[0], "doc", axis=0)

    near = [encoded] + [from_x(encoded, k) for k in (1, 2, 3)]
    swapped = other_half(encoded)
    row_q = queries.reshape(queries.shape[0], GROUP * HD)
    row_q = jnp.concatenate([row_q, swap_z(row_q, 2)], axis=0)
    far = [swapped] + [from_x(swapped, k) for k in (1, 2, 3)]
    all_q = [row_q] + [from_y(row_q, k) for k in (1, 2, 3)]

    kv_near = project(False, place, span_lens, near, weight)
    beside = swap_z(kv_near, 1)
    here = [kv_near, other_core(kv_near), beside, other_core(beside)]
    far = lax.optimization_barrier(far + all_q)[:4]
    kv_far = project(True, place, span_lens, far, weight)
    beside = swap_z(kv_far, 1)
    here += [kv_far, other_core(kv_far)]
    carries = attend_near(all_q, here)
    beside, carries, weights = lax.optimization_barrier((beside, carries, weights))
    kv_far = beside, other_core(beside)

    parts = [None] * 4
    for k in (2, 1, 3, 0):
        part = attend_far(k, place, carries, kv_far)
        parts[k] = from_y(part, -k) if k else part

    joint = fold(64, parts)
    own = fold(64, (joint, swap_z(joint, 2)), last=True)
    beside = swap_z(own, 1)
    rows = [own, beside, other_core(own), other_core(beside)]
    terms = output_terms(place, rows, weights)
    terms = [
        move(term, lambda y, z, c, x, h, j=j: (y + j, z, c, x + y, h))
        for j, term in enumerate(terms)
    ]
    mine, other = sum_terms(place, terms)
    other = other_half(other).astype(f32)
    return (residual.astype(f32) + (mine + other)).astype(bf16)


def solution(mesh):
    placed = (
        P(("doc", "span", "tp"), None),
        P(("doc", "span")),
        P(None, "tp", None),
        P(("doc", "span"), "tp", None),
        P("tp", None, ("doc", "span")),
        P("tp", ("doc", "span")),
    )
    return jax.shard_map(
        body, mesh=mesh, in_specs=placed, out_specs=P("tp", ("doc", "span")), check_vma=False
    )
```

```python
import functools

import jax
import jax.numpy as jnp
from jax import lax
from jax.experimental import pallas as pl
from jax.experimental.pallas import tpu as pltpu
from jax.sharding import PartitionSpec as P

SPAN = 64
HD = 128
GROUP = 8
AXES = ("doc", "span", "tp")
Z_ORDER = (0, 2, 1, 3)
EXP2_SCALE = HD**-0.5 * 1.4426950408889634
f32, bf16 = jnp.float32, jnp.bfloat16


def move(value, target):
    def index(y, z, c, x, h):
        return ((y % 4 * 4 + z % 4) * 2 + c % 2) * 8 + x % 4 * 2 + h % 2

    pairs = [
        (index(y, z, c, x, h), index(*target(y, z, c, x, h)))
        for y in range(4)
        for z in range(4)
        for c in range(2)
        for x in range(4)
        for h in range(2)
    ]
    return lax.ppermute(value, AXES, pairs)


def from_x(value, k):
    return move(value, lambda y, z, c, x, h: (y, z, c, x - k, h))


def from_y(value, k):
    return move(value, lambda y, z, c, x, h: (y - k, z, c, x, h))


def swap_z(value, step):
    return move(value, lambda y, z, c, x, h: (y, z ^ step, c, x, h))


def other_core(value):
    return move(value, lambda y, z, c, x, h: (y, z, c + 1, x, h))


def other_half(value):
    return move(value, lambda y, z, c, x, h: (y, z, c, x, h + 1))


def vmem(count):
    return [pl.BlockSpec(memory_space=pltpu.VMEM)] * count


ANY = pl.BlockSpec(memory_space=pl.ANY)
SMEM = pl.BlockSpec(memory_space=pltpu.SMEM)
OWN_COPIES = pltpu.CompilerParams(vmem_limit_bytes=60 * 1024 * 1024)
PARAMS = pltpu.CompilerParams(vmem_limit_bytes=40 * 1024 * 1024)


def cost(flops, nbytes, exps=0):
    return pl.CostEstimate(flops=flops, bytes_accessed=nbytes, transcendentals=exps)


def span_pair(place_ref, lens_ref, k, flip):
    x = place_ref[1]
    h = place_ref[2]
    half = (1 - h) if flip else h
    return (lax.rem(x + k, 4) * 2 + half) * 2


def project_kernel(flip, place_ref, lens_ref, e0, e1, e2, e3, weight, *rest):
    out = rest[-1]
    rows = lax.broadcasted_iota(jnp.int32, (SPAN, HD), 0)
    lane = lax.broadcasted_iota(jnp.int32, (16, 2 * HD), 1)
    lens = jnp.zeros((16, 2 * HD), f32)
    for k, block in enumerate((e0, e1, e2, e3)):
        both = jnp.dot(block[...], weight[...], preferred_element_type=f32)
        first = span_pair(place_ref, lens_ref, k, flip)
        for s in range(2):
            part = both[s * SPAN : (s + 1) * SPAN]
            valid = rows < lens_ref[first + s]
            keys = part[:, :HD]
            keys = jnp.where(valid, keys, keys[:1])
            values = jnp.where(valid, part[:, HD:], 0.0)
            at = k * 2 * SPAN + s * SPAN
            out[at : at + SPAN, :HD] = keys.astype(bf16)
            out[at : at + SPAN, HD:] = values.astype(bf16)
            lens = jnp.where(lane == 2 * k + s, lens_ref[first + s].astype(f32), lens)
    out[512:] = lens.astype(bf16)


def project(flip, place, lens, blocks, weight, after=()):
    return pl.pallas_call(
        functools.partial(project_kernel, flip),
        out_shape=jax.ShapeDtypeStruct((528, 2 * HD), bf16),
        in_specs=[SMEM, SMEM] + vmem(5) + [ANY] * len(after),
        out_specs=vmem(1)[0],
        compiler_params=PARAMS if flip else OWN_COPIES,
        cost_estimate=cost(2 * 512 * 1024 * 256, 2 << 20) if flip else cost(1024, 1024),
        name="project",
    )(place, lens, *blocks, weight, *after)


def split3(value):
    high = value.astype(bf16)
    rest = value - high.astype(f32)
    middle = rest.astype(bf16)
    low = (rest - middle.astype(f32)).astype(bf16)
    return high, middle, low


def put_stats(out, stats):
    terms = [term.astype(f32) for term in split3(stats)]
    lane = lax.broadcasted_iota(jnp.int32, stats.shape, 1)
    for i in (1, 2):
        shifted = pltpu.roll(terms[i], 2 * GROUP * i, axis=1)
        terms[0] = jnp.where(lane < 2 * GROUP * i, terms[0], shifted)
    out[:, GROUP * HD :] = terms[0].astype(bf16)


def get_stats(part):
    terms = part[:, GROUP * HD :].astype(f32)
    second, third = (pltpu.roll(terms, HD - 2 * GROUP * i, axis=1) for i in (1, 2))
    return (terms + second) + third


def attend_kernel(queries, parts, carries, valued, emit):
    rows = lax.broadcasted_iota(jnp.int32, (SPAN, HD), 0).astype(f32)
    for p, part in enumerate(parts):
        valued[p * 512 : (p + 1) * 512, :HD] = part[:512, HD:]
        lens = part[512:, :HD].astype(f32)
        for i in range(8):
            at = p * 512 + i * SPAN
            valid = rows < lens[:1, i : i + 1]
            valued[at : at + SPAN, HD:] = jnp.where(valid, 1.0, 0.0).astype(bf16)
    count = queries[0].shape[0]
    lane = lax.broadcasted_iota(jnp.int32, (count, HD), 1)
    step = 4
    tiles = [(i, g) for i in range(len(queries)) for g in range(0, GROUP, step)]

    def scores_of(i, g):
        q = jnp.concatenate(
            [queries[i][:, h * HD : (h + 1) * HD] for h in range(g, g + step)], axis=0
        )
        return [
            lax.dot_general(
                q, part[:512, :HD], (((1,), (1,)), ((), ())), preferred_element_type=f32
            )
            for part in parts
        ]

    ahead = scores_of(*tiles[0])
    for n, (i, g) in enumerate(tiles):
        scores = ahead
        if n + 1 < len(tiles):
            ahead = scores_of(*tiles[n + 1])
        if g == 0:
            packed = jnp.zeros((count, HD), f32)
            sums = [None] * GROUP
        top = functools.reduce(
            jnp.maximum,
            [block[:, a : a + HD] for block in scores for a in range(0, 512, HD)],
        )
        top = jnp.max(top, axis=-1, keepdims=True)
        if carries[i] is not None:
            before, before_stats = carries[i]
            old = jnp.concatenate([before_stats[:, h : h + 1] for h in range(g, g + step)], axis=0)
            top = jnp.maximum(top, old)
            shrink = jnp.exp2((old - top) * EXP2_SCALE)
        total = jnp.zeros((step * count, 2 * HD), f32)
        for p, block in enumerate(scores):
            probs = jnp.exp2((block - top) * EXP2_SCALE).astype(bf16)
            total += jnp.dot(
                probs, valued[p * 512 : (p + 1) * 512], preferred_element_type=f32
            )
        for j in range(step):
            h = g + j
            here = slice(j * count, (j + 1) * count)
            summed, weight = total[here, :HD], total[here, HD:]
            if carries[i] is not None:
                summed += before[:, h * HD : (h + 1) * HD] * shrink[here]
                weight += before_stats[:, GROUP + h : GROUP + h + 1] * shrink[here]
            sums[h] = summed
            packed = jnp.where(lane == h, top[here], packed)
            packed = jnp.where(lane == GROUP + h, weight, packed)
        if g + step == GROUP:
            emit(i, sums, packed)


def near_kernel(*refs):
    queries, parts = refs[:4], refs[4:-4]
    q_all, sums_all, stats_all, valued = refs[-4:]
    for i, q in enumerate(queries):
        q_all[i] = q[...]

    def emit(i, sums, packed):
        for h, value in enumerate(sums):
            sums_all[i, :, h * HD : (h + 1) * HD] = value
        stats_all[i] = packed

    attend_kernel(queries, parts, (None,) * 4, valued, emit)


def attend_near(queries, kv):
    count = queries[0].shape[0]
    return pl.pallas_call(
        near_kernel,
        out_shape=(
            jax.ShapeDtypeStruct((4, count, GROUP * HD), bf16),
            jax.ShapeDtypeStruct((4, count, GROUP * HD), f32),
            jax.ShapeDtypeStruct((4, count, HD), f32),
        ),
        in_specs=vmem(4 + len(kv)),
        out_specs=tuple(vmem(3)),
        scratch_shapes=[pltpu.VMEM((512 * len(kv), 2 * HD), bf16)],
        compiler_params=PARAMS,
        cost_estimate=cost(1024, 1024),
        name="attend_near",
    )(*queries, *kv)


def far_kernel(k, place_ref, q_all, sums_all, stats_all, *rest):
    parts, out, valued = rest[:-2], rest[-2], rest[-1]
    count = q_all.shape[1]
    at = lax.rem(place_ref[1] + k, 4)

    def emit(i, sums, packed):
        for h, value in enumerate(sums):
            out[:, h * HD : (h + 1) * HD] = value.astype(bf16)
        put_stats(out, packed)

    carry = (sums_all.at[at], stats_all[at])
    attend_kernel((q_all.at[at],), parts, (carry,), valued, emit)


def attend_far(k, place, carries, kv):
    q_all, sums_all, stats_all = carries
    count = q_all.shape[1]
    return pl.pallas_call(
        functools.partial(far_kernel, k),
        out_shape=jax.ShapeDtypeStruct((count, GROUP * HD + HD), bf16),
        in_specs=[SMEM] + vmem(3 + len(kv)),
        out_specs=vmem(1)[0],
        scratch_shapes=[pltpu.VMEM((512 * len(kv), 2 * HD), bf16)],
        compiler_params=PARAMS,
        cost_estimate=cost(4 * 512 * 1024 * 256, 2 << 20, 512 * 1024),
        name="attend_far",
    )(place, q_all, sums_all, stats_all, *kv)


def fold_kernel(last, *refs):
    parts, out = refs[:-1], refs[-1]
    stats = [get_stats(part) for part in parts]
    half = out.shape[0] // 2
    if last:
        stats[1] = jnp.concatenate([stats[1][half:], stats[1][:half]], axis=0)
    top = functools.reduce(jnp.maximum, stats)
    factors = [jnp.exp2((s - top) * EXP2_SCALE) for s in stats]
    shifted = [pltpu.roll(f, GROUP, axis=1) for f in factors]
    total = sum(f * s for f, s in zip(shifted, stats))
    if not last:
        lane = lax.broadcasted_iota(jnp.int32, top.shape, 1)
        put_stats(out, jnp.where(lane < GROUP, top, total))
    for g in range(GROUP):
        lanes = slice(g * HD, (g + 1) * HD)
        pieces = [part[:, lanes].astype(f32) for part in parts]
        if last:
            pieces[1] = jnp.concatenate([pieces[1][half:], pieces[1][:half]], axis=0)
        joint = sum(piece * f[:, g : g + 1] for piece, f in zip(pieces, factors))
        if last:
            joint = joint / total[:, GROUP + g : GROUP + g + 1]
        out[:, lanes] = joint.astype(bf16)


def fold(count, parts, last=False):
    return pl.pallas_call(
        functools.partial(fold_kernel, last),
        out_shape=jax.ShapeDtypeStruct((count, GROUP * HD + (0 if last else HD)), bf16),
        in_specs=vmem(len(parts)),
        out_specs=vmem(1)[0],
        compiler_params=PARAMS,
        cost_estimate=cost(8 * count * 1024, len(parts) * count << 11),
        name="fold",
    )(*parts)


def output_kernel(place_ref, r0, r1, r2, r3, weights, o0, o1, o2, o3, rows):
    y, z, c = place_ref[0], place_ref[3], place_ref[4]
    blocks = [r.at[i : i + 32] for r in (r0, r1, r2, r3) for i in (0, 32)]
    for i, block in enumerate(blocks):
        core = (1 - c) if i >= 4 else c
        at = (jnp.bitwise_xor(z, Z_ORDER[i % 4]) * 2 + core) * 32
        rows[pl.ds(pl.multiple_of(at, 32), 32), :] = block[...]
    for j, out in enumerate((o0, o1, o2, o3)):
        weight = weights[lax.rem(y + j, 4)]
        out[...] = jnp.dot(rows[...], weight, preferred_element_type=f32).astype(bf16)


def output_terms(place, rows, weights):
    return pl.pallas_call(
        output_kernel,
        out_shape=tuple([jax.ShapeDtypeStruct((256, 256), bf16)] * 4),
        in_specs=[SMEM] + vmem(5),
        out_specs=tuple(vmem(4)),
        scratch_shapes=[pltpu.VMEM((256, GROUP * HD), bf16)],
        compiler_params=PARAMS,
        cost_estimate=cost(2 * 256 * 1024 * 1024, 3 << 20),
        name="output",
    )(place, *rows, weights)


def sum_kernel(place_ref, t0, t1, t2, t3, mine, other):
    h = place_ref[2]
    for out, half in ((mine, h), (other, 1 - h)):
        at = pl.ds(pl.multiple_of(half * 128, 128), 128)
        out[...] = sum(t[at, :].astype(f32) for t in (t0, t1, t2, t3)).astype(out.dtype)


def sum_terms(place, terms):
    return pl.pallas_call(
        sum_kernel,
        out_shape=(
            jax.ShapeDtypeStruct((128, 256), f32),
            jax.ShapeDtypeStruct((128, 256), bf16),
        ),
        in_specs=[SMEM] + vmem(4),
        out_specs=tuple(vmem(2)),
        compiler_params=PARAMS,
        cost_estimate=cost(4 * 256 * 256, 1 << 19),
        name="sum_terms",
    )(place, *terms)


def body(encoded, span_lens, kv_weight, queries, out_weight, residual):
    span, tp = lax.axis_index("span"), lax.axis_index("tp")
    place = jnp.stack(
        [lax.axis_index("doc"), tp // 2, tp % 2, span // 2, span % 2]
    ).astype(jnp.int32)
    weight = kv_weight.reshape(kv_weight.shape[0], 2 * HD)
    weights = lax.all_gather(out_weight[0], "doc", axis=0)

    near = [encoded] + [from_x(encoded, k) for k in (1, 2, 3)]
    swapped = other_half(encoded)
    row_q = queries.reshape(queries.shape[0], GROUP * HD)
    row_q = jnp.concatenate([row_q, swap_z(row_q, 2)], axis=0)
    far = [swapped] + [from_x(swapped, k) for k in (1, 2, 3)]
    all_q = [row_q] + [from_y(row_q, k) for k in (1, 2, 3)]

    kv_near = project(False, place, span_lens, near, weight)
    beside = swap_z(kv_near, 1)
    here = [kv_near, other_core(kv_near), beside, other_core(beside)]
    far = lax.optimization_barrier(far + all_q)[:4]
    kv_far = project(True, place, span_lens, far, weight)
    beside = swap_z(kv_far, 1)
    here += [kv_far, other_core(kv_far)]
    carries = attend_near(all_q, here)
    beside, carries, weights = lax.optimization_barrier((beside, carries, weights))
    kv_far = beside, other_core(beside)

    parts = [None] * 4
    for k in (2, 1, 3, 0):
        part = attend_far(k, place, carries, kv_far)
        parts[k] = from_y(part, -k) if k else part

    joint = fold(64, parts)
    own = fold(64, (joint, swap_z(joint, 2)), last=True)
    beside = swap_z(own, 1)
    rows = [own, beside, other_core(own), other_core(beside)]
    terms = output_terms(place, rows, weights)
    terms = [
        move(term, lambda y, z, c, x, h, j=j: (y + j, z, c, x + y, h))
        for j, term in enumerate(terms)
    ]
    mine, other = sum_terms(place, terms)
    other = other_half(other).astype(f32)
    return (residual.astype(f32) + (mine + other)).astype(bf16)


def solution(mesh):
    placed = (
        P(("doc", "span", "tp"), None),
        P(("doc", "span")),
        P(None, "tp", None),
        P(("doc", "span"), "tp", None),
        P("tp", None, ("doc", "span")),
        P("tp", ("doc", "span")),
    )
    return jax.shard_map(
        body, mesh=mesh, in_specs=placed, out_specs=P("tp", ("doc", "span")), check_vma=False
    )
```
